32 devices in a mesh: pair: 8 (over z, x), virt: 4 (over y, core).
Axes of the slice: x: 2, y: 2, z: 4, core: 2. Of those that a mesh axis runs over, the one named last changes fastest.
Arguments:
- amplitudes: bfloat16 [16, 4, 8, 128], P('pair', None, 'virt'), may hold values from -6 to 6
- kept_groups: int32 [16, 4], P('pair'), may hold values from 0 to 7, all different within a row; in each aligned block of 2 rows (0 to 1, 2 to 3, ...) at most 2 rows name the same one
- tile_mask: int32 [16, 4, 2], P('pair'), may hold values 0 or 1
- owner_table: int32 [8], replicated, may hold values from 0 to 7, each once
- integrals: bfloat16 [1024, 1024], P('pair', 'virt'), may hold values from -0.25 to 0.25
- residual_in: bfloat16 [128, 1024], P('pair', 'virt'), may hold values from -6 to 6
- pair_energy: float32 [128], P('pair'), may hold values from -3 to -1
- virt_energy: float32 [1024], P('virt'), may hold values from 0.5 to 3
Outputs:
- update: float32 [128, 1024], P('pair', 'virt')
The draws below stay inside these ranges and needn't reach their ends.
Inputs may be any that keep to these rules, and one draw needn't show every extreme that they name: `kept_groups`: each block names 4 different tile groups; among the blocks of one index of pair each group is named at most 2 times. `owner_table`: a permutation of the tile groups.
All inputs are finite; a program needn't handle non-finite values. No bound on the sum of `tile_mask` on one device may be relied on, other than what follows from the above.
Results may differ from the reference program's by a relative error of at most 0.0003.
Values may be sent and summed in bfloat16 or wider, within the bound.
No kernel may reach another device: no remote copies, remote signals or barrier semaphores. Data moves between devices by JAX's collectives and lax.ppermute only.
A program may use at most 64 MiB of HBM per device.

```python
import math
import jax
import jax.numpy as jnp
import numpy as np
from jax import lax

TILE = 64
PAIRS = 8
CD_DEV = 2
BLK_DEV = 2
CAP = 2
KEEP = 4
NBLK = 16
NAB = 16
N_PAIR = 8


def touch_ends(result, rng, smallest, high):
    index_at = [jax.random.randint(jax.random.fold_in(rng, axis), (), 0, length) for axis, length in enumerate(result.shape)]
    longest = result.shape.index(max(result.shape))
    neighbour = index_at[:longest] + [(index_at[longest] + 1) % result.shape[longest]] + index_at[longest + 1:]
    return result.at[tuple(index_at)].set(smallest).at[tuple(neighbour)].set(high)


def levels(own_key, extent, split, least, top_value):
    level = 1.0
    for axis_at, shards_of in split:
        steps = jax.random.uniform(jax.random.fold_in(jax.random.fold_in(own_key, 6), axis_at), (shards_of,), jnp.float32, least / len(split), top_value / len(split))
        level = level * jnp.repeat(jnp.exp(steps), extent[axis_at] // shards_of).reshape((-1,) + (1,) * (len(extent) - 1 - axis_at))
    return level


def assign_block(key, own, number, rows, number_of, top, limit, skew):
    sequence = jax.random.permutation(key, number_of)
    packed, common = portions_of(number_of, rows * top, limit, skew, True), portions_of(number_of, rows * top, limit, skew, False)
    places = jnp.arange(number_of)

    def named(tallies, turn):
        used = int((tallies > 0).sum())
        fixed = max(1, used // 4)
        passed = fixed + (places - fixed + turn * (used - fixed)) % max(1, number_of - fixed)
        return jnp.zeros((number_of,), jnp.int32).at[sequence[jnp.where(places < fixed, places, passed)]].set(jnp.asarray(tallies, jnp.int32))

    tallies = jnp.where(number % 4 == 0, named(packed, number // 4), named(common, number - number // 4 - 1))
    mixed = jax.random.permutation(jax.random.fold_in(own, 3), number_of)
    giver, sink = mixed[0:number_of // 2 * 2:2], mixed[1:number_of // 2 * 2:2]
    slack = jnp.minimum(tallies[giver] - 1, limit - tallies[sink]) // 2
    slack = jnp.where((giver == sequence[0]) | (sink == sequence[0]) | (tallies[sink] == 0), 0, jnp.maximum(slack, 0))
    passed = jax.random.randint(jax.random.fold_in(own, 4), (number_of // 2,), 0, 1 << 20) % (slack + 1)
    tallies = tallies.at[giver].add(-passed).at[sink].add(passed)
    members = jnp.searchsorted(jnp.cumsum(tallies), jnp.arange(rows * top), side="right").astype(jnp.int32)
    listing = members.reshape(top, rows).T
    listing = listing[jax.random.permutation(jax.random.fold_in(own, 1), rows)]
    turn = jax.random.randint(jax.random.fold_in(own, 2), (rows, 1), 0, top)
    return jnp.take_along_axis(listing, (jnp.arange(top)[None, :] + turn) % top, axis=1)


def portions_of(number_of, total, bound, skew, full):
    weights = [(1 << 20) // math.isqrt(grade ** skew) + 1 for grade in range(1, number_of + 1)]
    largest = bound if full else min(bound, max(-(-total // number_of), total * weights[0] // sum(weights)))
    least = 1 if total - largest >= number_of - 1 else 0
    counts, spare = [largest] + [least] * (number_of - 1), total - largest - least * (number_of - 1)
    while spare > 0:
        movable = [i for i in range(1, number_of) if counts[i] < largest] or [i for i in range(1, number_of) if counts[i] < bound]
        mass, remaining = sum([weights[i] for i in movable]), spare
        for i in movable:
            addition = min(bound - counts[i], max(1, remaining * weights[i] // mass), spare)
            counts[i] = counts[i] + addition
            spare = spare - addition
    return np.array(counts)


def bell_draw(own_key, extent, scale, reach, pieces=(), kind=jnp.bfloat16):
    entries = jax.random.normal(own_key, extent, jnp.float32) * scale
    if len(pieces) > 0:
        entries = levels(own_key, extent, pieces, -0.22, 0.18) * entries
    return jnp.clip(entries, min=-reach, max=reach).astype(kind)


def setup_inputs(seed: int = 0) -> dict:
    key_of = jax.random.split(jax.random.key(seed), 9)
    amplitudes = bell_draw(key_of[0], (NBLK, KEEP, PAIRS, CD_DEV * TILE), 1.0, 6.0, ((0, 8), (2, 4)))
    kept_groups_keys = jax.random.split(jax.random.fold_in(key_of[1], 1), NBLK // BLK_DEV)
    kept_groups_turns = jax.random.permutation(jax.random.fold_in(key_of[1], 3), NBLK // BLK_DEV)
    kept_groups = jax.vmap(lambda own, number: assign_block(jax.random.fold_in(key_of[1], 2), own, number, BLK_DEV, N_PAIR, KEEP, CAP, 2))(kept_groups_keys, kept_groups_turns).reshape((NBLK, KEEP))
    tile_mask = touch_ends((jax.random.randint(key_of[2], (NBLK, KEEP, CD_DEV), 0, 4) < 3).astype(jnp.int32), jax.random.fold_in(key_of[2], 1), 0, 1)
    owner_table = jax.random.permutation(key_of[3], N_PAIR).astype(jnp.int32)
    integrals = bell_draw(key_of[4], (N_PAIR * CD_DEV * TILE, NAB * TILE), (KEEP * CD_DEV * TILE) ** -0.5, 0.25, ((0, 8), (1, 4)))
    residual_in = bell_draw(key_of[5], (NBLK * PAIRS, NAB * TILE), 1.0, 6.0, ((0, 8), (1, 4)))
    pair_energy = jnp.clip(-3.0 + 2.0 * jax.random.uniform(key_of[6], (NBLK * PAIRS,), jnp.float32) ** levels(key_of[6], (NBLK * PAIRS,), ((0, 8),), -0.2, 0.2), -3.0, -1.0)
    virt_energy = jnp.clip(0.5 + 2.5 * jax.random.uniform(key_of[7], (NAB * TILE,), jnp.float32) ** levels(key_of[7], (NAB * TILE,), ((0, 4),), -0.2, 0.2), 0.5, 3.0)
    return dict(amplitudes=amplitudes, kept_groups=kept_groups, tile_mask=tile_mask, owner_table=owner_table, integrals=integrals, residual_in=residual_in, pair_energy=pair_energy, virt_energy=virt_energy)


def reference(amplitudes, kept_groups, tile_mask, owner_table, integrals, residual_in, pair_energy, virt_energy):
    group_width = CD_DEV * TILE
    tile_keep = jnp.repeat(tile_mask, TILE, axis=2).astype(amplitudes.dtype)
    kept_amplitudes = amplitudes * tile_keep[:, :, None, :]
    owner_slots = owner_table[kept_groups].astype(jnp.int32)
    offsets = jnp.arange(group_width, dtype=jnp.int32)

    def one_block(items):
        amplitude, slot_row = items
        row_index = (slot_row[:, None] * group_width + offsets[None, :]).reshape(-1).astype(jnp.int32)
        block_rows = jnp.take(integrals, row_index, axis=0)
        left_rows = jnp.transpose(amplitude, (1, 0, 2)).reshape(PAIRS, KEEP * group_width)
        return jnp.dot(left_rows, block_rows, preferred_element_type=jnp.float32)

    ladder = lax.map(one_block, (kept_amplitudes, owner_slots)).reshape(NBLK * PAIRS, NAB * TILE)
    denominator = pair_energy[:, None] - virt_energy[None, :]
    return (residual_in.astype(jnp.float32) + ladder) / denominator
```

```python
import functools
import math

import jax
import jax.numpy as jnp
from jax import lax
from jax.experimental import pallas as pl
from jax.experimental.pallas import tpu as pltpu
from jax.sharding import PartitionSpec as P

OUTER_BIT = 0


def relative_place(slot, me, bits):
    apart = slot ^ me
    place = jnp.int32(0)
    for at, bit in enumerate(bits):
        place = place | (((apart >> bit) & 1) << at)
    return place


def spread_kernel(bits, kept_ref, mask_ref, owner_ref, amp_ref, out_ref, rows_ref):
    blocks, keep, pair_rows, width = amp_ref.shape
    tiles = mask_ref.shape[1]
    me = lax.axis_index("pair")
    lane_tile = lax.broadcasted_iota(jnp.int32, (pair_rows, width), 1) // (width // tiles)
    out_rows = out_ref.shape[0]
    tasks = blocks * keep
    row = lax.broadcasted_iota(jnp.int32, (out_rows, tasks * pair_rows), 0)
    column = lax.broadcasted_iota(jnp.int32, (out_rows, tasks * pair_rows), 1)
    wanted = jnp.full((out_rows, tasks * pair_rows), -1, jnp.int32)
    for b in range(blocks):
        for k in range(keep):
            task = b * keep + k
            place = relative_place(owner_ref[kept_ref[b, k]], me, bits)
            first = (place * blocks + b) * pair_rows
            wanted = jnp.where(column // pair_rows == task, first + column % pair_rows, wanted)
            scale = jnp.zeros((pair_rows, width), jnp.float32)
            for s in range(tiles):
                scale = jnp.where(lane_tile == s, mask_ref[b, s, k].astype(jnp.float32), scale)
            rows_ref[pl.ds(task * pair_rows, pair_rows), :] = amp_ref[b, k].astype(jnp.float32) * scale
    pick = (row == wanted).astype(jnp.bfloat16)
    out_ref[...] = jnp.dot(
        pick, rows_ref[...].astype(jnp.bfloat16), preferred_element_type=jnp.float32
    ).astype(out_ref.dtype)


def spread(amplitudes, kept_groups, tile_mask, owner_table, bits):
    blocks, keep, pair_rows, width = amplitudes.shape
    out_rows = owner_table.shape[0] * blocks * pair_rows
    smem = pl.BlockSpec(memory_space=pltpu.SMEM)
    vmem = pl.BlockSpec(memory_space=pltpu.VMEM)
    return pl.pallas_call(
        functools.partial(spread_kernel, bits),
        out_shape=jax.ShapeDtypeStruct((out_rows, width), amplitudes.dtype),
        in_specs=[smem, smem, smem, vmem],
        out_specs=vmem,
        scratch_shapes=[pltpu.VMEM((blocks * keep * pair_rows, width), jnp.float32)],
        name="spread",
    )(kept_groups, jnp.swapaxes(tile_mask, 1, 2), owner_table, amplitudes)


def share_of(blocks, pair_rows, lhs, blocks_of_integrals):
    virt_size = lhs.shape[0] // (len(blocks_of_integrals) * blocks * pair_rows)
    full_rows = virt_size * pair_rows
    inner = len(blocks_of_integrals)
    me = lax.axis_index("virt")
    row = lax.broadcasted_iota(jnp.int32, (blocks * full_rows, lhs.shape[0]), 0)
    column = lax.broadcasted_iota(jnp.int32, (blocks * full_rows, lhs.shape[0]), 1)
    block, pair = row // full_rows, row % full_rows
    piece = (pair // pair_rows) ^ me
    total = None
    for t in range(inner):
        wanted = ((piece * inner + t) * blocks + block) * pair_rows + pair % pair_rows
        pick = (column == wanted).astype(jnp.bfloat16)
        left = jnp.dot(pick, lhs, preferred_element_type=jnp.float32).astype(jnp.bfloat16)
        term = jnp.dot(left, blocks_of_integrals[t], preferred_element_type=jnp.float32)
        total = term if total is None else total + term
    return total


def far_kernel(blocks, pair_rows, lhs_ref, *refs):
    *integral_refs, out_ref = refs
    held = [r[t] for r in integral_refs for t in range(r.shape[0])]
    out_ref[...] = share_of(blocks, pair_rows, lhs_ref[...], held)


def near_kernel(blocks, pair_rows, lhs_ref, residual_ref, pair_ref, virt_ref, *refs):
    *integral_refs, top_ref, under_ref = refs
    held = [r[t] for r in integral_refs for t in range(r.shape[0])]
    total = share_of(blocks, pair_rows, lhs_ref[...], held)
    top_ref[...] = residual_ref[...].astype(jnp.float32) + total
    rows = total.shape[0]
    here = lax.broadcasted_iota(jnp.int32, (rows, rows), 0)
    there = lax.broadcasted_iota(jnp.int32, (rows, rows), 1)
    pair_column = jnp.sum(jnp.where(here == there, pair_ref[...], 0.0), axis=1, keepdims=True)
    under_ref[...] = pair_column - virt_ref[...]


def swap(x, axis_name, bit):
    size = lax.axis_size(axis_name)
    return lax.ppermute(x, axis_name, [(i, i ^ (1 << bit)) for i in range(size)])


def local(
    amplitudes,
    kept_groups,
    tile_mask,
    owner_table,
    integrals,
    residual_in,
    pair_energy,
    virt_energy,
):
    blocks, _, pair_rows, width = amplitudes.shape
    columns = integrals.shape[1]
    pair_bits = (lax.axis_size("pair") - 1).bit_length()
    virt_bits = (lax.axis_size("virt") - 1).bit_length()
    inner_bits = [b for b in reversed(range(pair_bits)) if b != OUTER_BIT]
    bits = tuple(inner_bits) + (OUTER_BIT,)
    vmem = pl.BlockSpec(memory_space=pltpu.VMEM)

    held = integrals[None]
    spread_rows = spread(amplitudes, kept_groups, tile_mask, owner_table, bits)
    half = spread_rows.shape[0] // 2
    pieces = spread_rows.reshape(2, half, width)
    for bit in inner_bits:
        held = jnp.concatenate([held, swap(held, "pair", bit)], axis=0)
    for bit in range(virt_bits):
        pieces = jnp.concatenate([pieces, swap(pieces, "virt", bit)], axis=1)
    far_rows = swap(pieces[1], "pair", OUTER_BIT)
    rows = residual_in.shape[0]
    far = pl.pallas_call(
        functools.partial(far_kernel, blocks, pair_rows),
        out_shape=jax.ShapeDtypeStruct((rows, columns), jnp.float32),
        in_specs=[vmem] * 2,
        out_specs=vmem,
        name="far",
    )(far_rows, held)
    top, under = pl.pallas_call(
        functools.partial(near_kernel, blocks, pair_rows),
        out_shape=[jax.ShapeDtypeStruct((rows, columns), jnp.float32)] * 2,
        in_specs=[vmem] * 5,
        out_specs=[vmem] * 2,
        name="near",
    )(pieces[0], residual_in, pair_energy[None, :], virt_energy[None, :], held)
    return (top + swap(far, "pair", OUTER_BIT)) / under


def general(
    amplitudes,
    kept_groups,
    tile_mask,
    owner_table,
    integrals,
    residual_in,
    pair_energy,
    virt_energy,
):
    block_count = amplitudes.shape[0]
    keep_count = amplitudes.shape[1]
    pair_rows = amplitudes.shape[2]
    group_width = amplitudes.shape[3]
    column_count = integrals.shape[1]
    tile_width = group_width // tile_mask.shape[2]
    group_total = owner_table.shape[0]
    tile_keep = jnp.repeat(tile_mask.astype(amplitudes.dtype), tile_width, axis=2)
    kept_amplitudes = amplitudes * tile_keep[:, :, None, :]
    group_match = kept_groups[:, :, None] == jnp.arange(group_total, dtype=jnp.int32)[None, None, :]
    owner_slots = jnp.sum(jnp.where(group_match, owner_table[None, None, :], 0), axis=2)
    placing = owner_slots[:, None, :] == jnp.arange(group_total, dtype=jnp.int32)[None, :, None]
    outgoing = jnp.einsum(
        "bqk,bkrw->qbrw", placing.astype(jnp.bfloat16), kept_amplitudes, preferred_element_type=jnp.float32
    ).astype(jnp.bfloat16)
    full_pairs = pair_rows * lax.axis_size("virt")
    arrived = lax.all_to_all(outgoing, "pair", split_axis=0, concat_axis=0, tiled=True)
    assembled = lax.all_gather(arrived, "virt", axis=2, tiled=True)
    partial_value = jnp.dot(
        assembled.reshape(-1, group_width), integrals, preferred_element_type=jnp.float32
    )
    ladder = lax.psum_scatter(partial_value, "pair", scatter_dimension=0, tiled=True)
    denominator = pair_energy[:, None] - virt_energy[None, :]
    return (residual_in.astype(jnp.float32) + ladder) / denominator


def solution(mesh):
    sizes = dict(mesh.shape)
    regular = all(s & (s - 1) == 0 for s in sizes.values()) and sizes["pair"] <= 8
    return jax.shard_map(
        local if regular else general,
        mesh=mesh,
        in_specs=(
            P("pair", None, "virt", None),
            P("pair", None),
            P("pair", None, None),
            P(),
            P("pair", "virt"),
            P("pair", "virt"),
            P("pair"),
            P("virt"),
        ),
        out_specs=P("pair", "virt"),
        check_vma=False,
    )
```

```python
import functools
import math

import jax
import jax.numpy as jnp
from jax import lax
from jax.experimental import pallas as pl
from jax.experimental.pallas import tpu as pltpu
from jax.sharding import PartitionSpec as P

KERNEL_VMEM = 1 << 20
STEPS = [(4, [0]), (1, [0, 4]), (2, [0, 4]), (3, [0, 4])]


def prepare_kernel(
    kept_hbm,
    mask_hbm,
    owner_hbm,
    amp_hbm,
    integrals_hbm,
    residual_hbm,
    pair_hbm,
    virt_hbm,
    rows_ref,
    own_ref,
    residual_ref,
    under_ref,
    kept_ref,
    mask_ref,
    owner_ref,
    amp_ref,
    rest_ref,
    pair_ref,
    virt_ref,
    kept_rows_ref,
    sems,
):
    moves = [
        pltpu.make_async_copy(source, target, sems.at[n])
        for n, (source, target) in enumerate(
            (
                (kept_hbm, kept_ref),
                (mask_hbm, mask_ref),
                (owner_hbm, owner_ref),
                (amp_hbm, amp_ref),
                (integrals_hbm, own_ref.at[0]),
                (residual_hbm, rest_ref),
                (pair_hbm, pair_ref),
                (virt_hbm, virt_ref),
            )
        )
    ]
    for move in moves:
        move.start()
    blocks, keep, pair_rows, width = amp_ref.shape
    tiles = mask_ref.shape[1]
    me = lax.axis_index("pair")
    lane_tile = lax.broadcasted_iota(jnp.int32, (pair_rows, width), 1) // (width // tiles)
    out_rows = rows_ref.shape[0]
    tasks = blocks * keep
    row = lax.broadcasted_iota(jnp.int32, (out_rows, tasks * pair_rows), 0)
    column = lax.broadcasted_iota(jnp.int32, (out_rows, tasks * pair_rows), 1)
    wanted = jnp.full((out_rows, tasks * pair_rows), -1, jnp.int32)
    for move in moves:
        move.wait()
    for b in range(blocks):
        for k in range(keep):
            task = b * keep + k
            first = ((owner_ref[kept_ref[b, k]] ^ me) * blocks + b) * pair_rows
            wanted = jnp.where(column // pair_rows == task, first + column % pair_rows, wanted)
            scale = jnp.zeros((pair_rows, width), jnp.float32)
            for s in range(tiles):
                scale = jnp.where(lane_tile == s, mask_ref[b, s, k].astype(jnp.float32), scale)
            kept_rows_ref[pl.ds(task * pair_rows, pair_rows), :] = amp_ref[b, k].astype(jnp.float32) * scale
    pick = (row == wanted).astype(jnp.bfloat16)
    rows_ref[...] = jnp.dot(
        pick, kept_rows_ref[...].astype(jnp.bfloat16), preferred_element_type=jnp.float32
    ).astype(rows_ref.dtype)
    residual_ref[...] = rest_ref[...].astype(jnp.float32)
    count = under_ref.shape[0]
    here = lax.broadcasted_iota(jnp.int32, (count, count), 0)
    there = lax.broadcasted_iota(jnp.int32, (count, count), 1)
    pair_column = jnp.sum(jnp.where(here == there, pair_ref[...], 0.0), axis=1, keepdims=True)
    under_ref[...] = pair_column - virt_ref[...]


def prepare(amplitudes, kept_groups, tile_mask, owner_table, integrals, residual_in, pair_energy, virt_energy):
    blocks, keep, pair_rows, width = amplitudes.shape
    out_rows = owner_table.shape[0] * blocks * pair_rows
    operands = (
        kept_groups,
        jnp.swapaxes(tile_mask, 1, 2),
        owner_table,
        amplitudes,
        integrals,
        residual_in,
        pair_energy[None, :],
        virt_energy[None, :],
    )
    operands = [pltpu.with_memory_space_constraint(x, pltpu.HBM) for x in operands]
    scratch = [pltpu.SMEM(x.shape, x.dtype) for x in operands[:3]]
    scratch += [pltpu.VMEM(x.shape, x.dtype) for x in (operands[3], *operands[5:])]
    return pl.pallas_call(
        prepare_kernel,
        out_shape=[
            jax.ShapeDtypeStruct((out_rows, width), amplitudes.dtype),
            jax.ShapeDtypeStruct((1, *integrals.shape), integrals.dtype),
            jax.ShapeDtypeStruct(residual_in.shape, jnp.float32),
            jax.ShapeDtypeStruct(residual_in.shape, jnp.float32),
        ],
        in_specs=[pl.BlockSpec(memory_space=pl.ANY)] * len(operands),
        out_specs=[pl.BlockSpec(memory_space=pltpu.VMEM)] * 4,
        scratch_shapes=scratch
        + [pltpu.VMEM((blocks * keep * pair_rows, width), jnp.float32), pltpu.SemaphoreType.DMA((len(operands),))],
        compiler_params=pltpu.CompilerParams(vmem_limit_bytes=KERNEL_VMEM),
        name="prepare",
    )(*operands)


def share_of(blocks, pair_rows, lhs, blocks_of_integrals):
    virt_size = lhs.shape[0] // (len(blocks_of_integrals) * blocks * pair_rows)
    full_rows = virt_size * pair_rows
    count = len(blocks_of_integrals)
    me = lax.axis_index("virt")
    row = lax.broadcasted_iota(jnp.int32, (blocks * full_rows, lhs.shape[0]), 0)
    column = lax.broadcasted_iota(jnp.int32, (blocks * full_rows, lhs.shape[0]), 1)
    block, pair = row // full_rows, row % full_rows
    piece = (pair // pair_rows) ^ me
    total = None
    for t in range(count):
        wanted = ((piece * count + t) * blocks + block) * pair_rows + pair % pair_rows
        pick = (column == wanted).astype(jnp.bfloat16)
        left = jnp.dot(pick, lhs, preferred_element_type=jnp.float32).astype(jnp.bfloat16)
        term = jnp.dot(left, blocks_of_integrals[t], preferred_element_type=jnp.float32)
        total = term if total is None else total + term
    return total


def update_kernel(blocks, pair_rows, places, lhs_ref, residual_ref, under_ref, *refs):
    *integral_refs, out_ref = refs
    held = [None] * sum(len(p) for p in places)
    for ref, at in zip(integral_refs, places):
        for t, place in enumerate(at):
            held[place] = ref[t]
    total = share_of(blocks, pair_rows, lhs_ref[...], held)
    out_ref[...] = (residual_ref[...] + total) / under_ref[...]


def swap(x, axis_name, mask):
    size = lax.axis_size(axis_name)
    return lax.ppermute(x, axis_name, [(i, i ^ mask) for i in range(size)])


def local(
    amplitudes,
    kept_groups,
    tile_mask,
    owner_table,
    integrals,
    residual_in,
    pair_energy,
    virt_energy,
):
    blocks, _, pair_rows, _ = amplitudes.shape
    vmem = pl.BlockSpec(memory_space=pltpu.VMEM)
    virt_bits = (lax.axis_size("virt") - 1).bit_length()
    rows, own, residual, under = prepare(
        amplitudes, kept_groups, tile_mask, owner_table, integrals, residual_in, pair_energy, virt_energy
    )
    have = {0: own}
    arrays = [(own, (0,))]
    for mask, labels in STEPS:
        sent = [have[l] if (l or len(labels) > 1) else integrals[None] for l in labels]
        sent = sent[0] if len(sent) == 1 else jnp.concatenate(sent, axis=0)
        got = swap(sent, "pair", mask)
        arrays.append((got, tuple(l ^ mask for l in labels)))
        for n, l in enumerate(labels):
            have[l ^ mask] = got if len(labels) == 1 else got[n : n + 1]
    pieces = rows
    for bit in range(virt_bits):
        pieces = jnp.concatenate([pieces, swap(pieces, "virt", 1 << bit)], axis=0)
    return pl.pallas_call(
        functools.partial(update_kernel, blocks, pair_rows, [at for _, at in arrays]),
        out_shape=jax.ShapeDtypeStruct(residual_in.shape, jnp.float32),
        in_specs=[vmem] * (3 + len(arrays)),
        out_specs=vmem,
        compiler_params=pltpu.CompilerParams(vmem_limit_bytes=KERNEL_VMEM),
        name="update",
    )(pieces, residual, under, *[x for x, _ in arrays])


def general(
    amplitudes,
    kept_groups,
    tile_mask,
    owner_table,
    integrals,
    residual_in,
    pair_energy,
    virt_energy,
):
    block_count = amplitudes.shape[0]
    keep_count = amplitudes.shape[1]
    pair_rows = amplitudes.shape[2]
    group_width = amplitudes.shape[3]
    column_count = integrals.shape[1]
    tile_width = group_width // tile_mask.shape[2]
    group_total = owner_table.shape[0]
    tile_keep = jnp.repeat(tile_mask.astype(amplitudes.dtype), tile_width, axis=2)
    kept_amplitudes = amplitudes * tile_keep[:, :, None, :]
    group_match = kept_groups[:, :, None] == jnp.arange(group_total, dtype=jnp.int32)[None, None, :]
    owner_slots = jnp.sum(jnp.where(group_match, owner_table[None, None, :], 0), axis=2)
    placing = owner_slots[:, None, :] == jnp.arange(group_total, dtype=jnp.int32)[None, :, None]
    outgoing = jnp.einsum(
        "bqk,bkrw->qbrw", placing.astype(jnp.bfloat16), kept_amplitudes, preferred_element_type=jnp.float32
    ).astype(jnp.bfloat16)
    full_pairs = pair_rows * lax.axis_size("virt")
    arrived = lax.all_to_all(outgoing, "pair", split_axis=0, concat_axis=0, tiled=True)
    assembled = lax.all_gather(arrived, "virt", axis=2, tiled=True)
    partial_value = jnp.dot(
        assembled.reshape(-1, group_width), integrals, preferred_element_type=jnp.float32
    )
    ladder = lax.psum_scatter(partial_value, "pair", scatter_dimension=0, tiled=True)
    denominator = pair_energy[:, None] - virt_energy[None, :]
    return (residual_in.astype(jnp.float32) + ladder) / denominator


def solution(mesh):
    sizes = dict(mesh.shape)
    regular = all(s & (s - 1) == 0 for s in sizes.values()) and sizes["pair"] <= 8
    return jax.shard_map(
        local if regular else general,
        mesh=mesh,
        in_specs=(
            P("pair", None, "virt", None),
            P("pair", None),
            P("pair", None, None),
            P(),
            P("pair", "virt"),
            P("pair", "virt"),
            P("pair"),
            P("virt"),
        ),
        out_specs=P("pair", "virt"),
        check_vma=False,
    )
```

```python
import functools
import math

import jax
import jax.numpy as jnp
from jax import lax
from jax.experimental import pallas as pl
from jax.experimental.pallas import tpu as pltpu
from jax.sharding import PartitionSpec as P

KERNEL_VMEM = 1 << 20


def prepare_kernel(
    kept_hbm,
    mask_hbm,
    owner_hbm,
    amp_hbm,
    integrals_hbm,
    residual_hbm,
    pair_hbm,
    virt_hbm,
    rows_ref,
    own_ref,
    residual_ref,
    under_ref,
    kept_ref,
    mask_ref,
    owner_ref,
    amp_ref,
    rest_ref,
    pair_ref,
    virt_ref,
    kept_rows_ref,
    sems,
):
    moves = [
        pltpu.make_async_copy(source, target, sems.at[n])
        for n, (source, target) in enumerate(
            (
                (kept_hbm, kept_ref),
                (mask_hbm, mask_ref),
                (owner_hbm, owner_ref),
                (amp_hbm, amp_ref),
                (integrals_hbm, own_ref.at[0]),
                (residual_hbm, rest_ref),
                (pair_hbm, pair_ref),
                (virt_hbm, virt_ref),
            )
        )
    ]
    for move in moves:
        move.start()
    blocks, keep, pair_rows, width = amp_ref.shape
    tiles = mask_ref.shape[1]
    me = lax.axis_index("pair")
    lane_tile = lax.broadcasted_iota(jnp.int32, (pair_rows, width), 1) // (width // tiles)
    out_rows = rows_ref.shape[0]
    tasks = blocks * keep
    row = lax.broadcasted_iota(jnp.int32, (out_rows, tasks * pair_rows), 0)
    column = lax.broadcasted_iota(jnp.int32, (out_rows, tasks * pair_rows), 1)
    wanted = jnp.full((out_rows, tasks * pair_rows), -1, jnp.int32)
    for move in moves:
        move.wait()
    for b in range(blocks):
        for k in range(keep):
            task = b * keep + k
            first = ((owner_ref[kept_ref[b, k]] ^ me) * blocks + b) * pair_rows
            wanted = jnp.where(column // pair_rows == task, first + column % pair_rows, wanted)
            scale = jnp.zeros((pair_rows, width), jnp.float32)
            for s in range(tiles):
                scale = jnp.where(lane_tile == s, mask_ref[b, s, k].astype(jnp.float32), scale)
            kept_rows_ref[pl.ds(task * pair_rows, pair_rows), :] = amp_ref[b, k].astype(jnp.float32) * scale
    pick = (row == wanted).astype(jnp.bfloat16)
    rows_ref[...] = jnp.dot(
        pick, kept_rows_ref[...].astype(jnp.bfloat16), preferred_element_type=jnp.float32
    ).astype(rows_ref.dtype)
    residual_ref[...] = rest_ref[...].astype(jnp.float32)
    count = under_ref.shape[0]
    here = lax.broadcasted_iota(jnp.int32, (count, count), 0)
    there = lax.broadcasted_iota(jnp.int32, (count, count), 1)
    pair_column = jnp.sum(jnp.where(here == there, pair_ref[...], 0.0), axis=1, keepdims=True)
    under_ref[...] = pair_column - virt_ref[...]


def prepare(amplitudes, kept_groups, tile_mask, owner_table, integrals, residual_in, pair_energy, virt_energy):
    blocks, keep, pair_rows, width = amplitudes.shape
    out_rows = owner_table.shape[0] * blocks * pair_rows
    operands = (
        kept_groups,
        jnp.swapaxes(tile_mask, 1, 2),
        owner_table,
        amplitudes,
        integrals,
        residual_in,
        pair_energy[None, :],
        virt_energy[None, :],
    )
    operands = [pltpu.with_memory_space_constraint(x, pltpu.HBM) for x in operands]
    scratch = [pltpu.SMEM(x.shape, x.dtype) for x in operands[:3]]
    scratch += [pltpu.VMEM(x.shape, x.dtype) for x in (operands[3], *operands[5:])]
    return pl.pallas_call(
        prepare_kernel,
        out_shape=[
            jax.ShapeDtypeStruct((out_rows, width), amplitudes.dtype),
            jax.ShapeDtypeStruct((1, *integrals.shape), integrals.dtype),
            jax.ShapeDtypeStruct(residual_in.shape, jnp.float32),
            jax.ShapeDtypeStruct(residual_in.shape, jnp.float32),
        ],
        in_specs=[pl.BlockSpec(memory_space=pl.ANY)] * len(operands),
        out_specs=[pl.BlockSpec(memory_space=pltpu.VMEM)] * 4,
        scratch_shapes=scratch
        + [pltpu.VMEM((blocks * keep * pair_rows, width), jnp.float32), pltpu.SemaphoreType.DMA((len(operands),))],
        compiler_params=pltpu.CompilerParams(vmem_limit_bytes=KERNEL_VMEM),
        name="prepare",
    )(*operands)


def arrange_kernel(blocks, pair_rows, order, rows_ref, out_ref):
    count, out_rows, _ = out_ref.shape
    full_rows = len(order) * pair_rows
    me = lax.axis_index("virt")
    row = lax.broadcasted_iota(jnp.int32, (out_rows, rows_ref.shape[0]), 0)
    column = lax.broadcasted_iota(jnp.int32, (out_rows, rows_ref.shape[0]), 1)
    block, pair = row // full_rows, row % full_rows
    apart = (pair // pair_rows) ^ me
    piece = sum(jnp.where(apart == mask, n, 0) for n, mask in enumerate(order))
    rows = rows_ref[...]
    for t in range(count):
        wanted = ((piece * count + t) * blocks + block) * pair_rows + pair % pair_rows
        pick = (column == wanted).astype(jnp.bfloat16)
        out_ref[t] = jnp.dot(pick, rows, preferred_element_type=jnp.float32).astype(out_ref.dtype)


def update_kernel(places, rows_ref, residual_ref, under_ref, *refs):
    *integral_refs, out_ref = refs
    total = residual_ref[...]
    for ref, at in zip(integral_refs, places):
        for t, place in enumerate(at):
            total += jnp.dot(rows_ref[place], ref[t], preferred_element_type=jnp.float32)
    out_ref[...] = total / under_ref[...]


def swap(x, pair_mask, virt_mask):
    pair_size, virt_size = lax.axis_size("pair"), lax.axis_size("virt")
    moves = [
        (p * virt_size + v, (p ^ pair_mask) * virt_size + (v ^ virt_mask))
        for p in range(pair_size)
        for v in range(virt_size)
    ]
    return lax.ppermute(x, ("pair", "virt"), moves)


def local(
    amplitudes,
    kept_groups,
    tile_mask,
    owner_table,
    integrals,
    residual_in,
    pair_energy,
    virt_energy,
):
    blocks, _, pair_rows, _ = amplitudes.shape
    vmem = pl.BlockSpec(memory_space=pltpu.VMEM)
    virt_size = lax.axis_size("virt")
    rows, own, residual, under = prepare(
        amplitudes, kept_groups, tile_mask, owner_table, integrals, residual_in, pair_energy, virt_energy
    )
    far = swap(integrals[None], 4, 0)
    arrays = [(own, (0,)), (far, (4,))]
    both = jnp.concatenate([own, far], axis=0)
    for mask in (2, 3, 1):
        arrays.append((swap(both, mask, 0), (mask, mask ^ 4)))
    pieces, order = rows, [0]
    for mask in (1, 2):
        pieces = jnp.concatenate([pieces, swap(pieces, 0, mask)], axis=0)
        order = order + [at ^ mask for at in order]
    count = owner_table.shape[0]
    slabs = pl.pallas_call(
        functools.partial(arrange_kernel, blocks, pair_rows, order),
        out_shape=jax.ShapeDtypeStruct((count, residual_in.shape[0], pieces.shape[1]), pieces.dtype),
        in_specs=[vmem],
        out_specs=vmem,
        compiler_params=pltpu.CompilerParams(vmem_limit_bytes=KERNEL_VMEM),
        name="arrange",
    )(pieces)
    return pl.pallas_call(
        functools.partial(update_kernel, [at for _, at in arrays]),
        out_shape=jax.ShapeDtypeStruct(residual_in.shape, jnp.float32),
        in_specs=[vmem] * (3 + len(arrays)),
        out_specs=vmem,
        compiler_params=pltpu.CompilerParams(vmem_limit_bytes=KERNEL_VMEM),
        name="update",
    )(slabs, residual, under, *[x for x, _ in arrays])


def general(
    amplitudes,
    kept_groups,
    tile_mask,
    owner_table,
    integrals,
    residual_in,
    pair_energy,
    virt_energy,
):
    block_count = amplitudes.shape[0]
    keep_count = amplitudes.shape[1]
    pair_rows = amplitudes.shape[2]
    group_width = amplitudes.shape[3]
    column_count = integrals.shape[1]
    tile_width = group_width // tile_mask.shape[2]
    group_total = owner_table.shape[0]
    tile_keep = jnp.repeat(tile_mask.astype(amplitudes.dtype), tile_width, axis=2)
    kept_amplitudes = amplitudes * tile_keep[:, :, None, :]
    group_match = kept_groups[:, :, None] == jnp.arange(group_total, dtype=jnp.int32)[None, None, :]
    owner_slots = jnp.sum(jnp.where(group_match, owner_table[None, None, :], 0), axis=2)
    placing = owner_slots[:, None, :] == jnp.arange(group_total, dtype=jnp.int32)[None, :, None]
    outgoing = jnp.einsum(
        "bqk,bkrw->qbrw", placing.astype(jnp.bfloat16), kept_amplitudes, preferred_element_type=jnp.float32
    ).astype(jnp.bfloat16)
    full_pairs = pair_rows * lax.axis_size("virt")
    arrived = lax.all_to_all(outgoing, "pair", split_axis=0, concat_axis=0, tiled=True)
    assembled = lax.all_gather(arrived, "virt", axis=2, tiled=True)
    partial_value = jnp.dot(
        assembled.reshape(-1, group_width), integrals, preferred_element_type=jnp.float32
    )
    ladder = lax.psum_scatter(partial_value, "pair", scatter_dimension=0, tiled=True)
    denominator = pair_energy[:, None] - virt_energy[None, :]
    return (residual_in.astype(jnp.float32) + ladder) / denominator


def solution(mesh):
    sizes = dict(mesh.shape)
    regular = all(s & (s - 1) == 0 for s in sizes.values()) and sizes["pair"] <= 8
    return jax.shard_map(
        local if regular else general,
        mesh=mesh,
        in_specs=(
            P("pair", None, "virt", None),
            P("pair", None),
            P("pair", None, None),
            P(),
            P("pair", "virt"),
            P("pair", "virt"),
            P("pair"),
            P("virt"),
        ),
        out_specs=P("pair", "virt"),
        check_vma=False,
    )
```

```python
import functools

import jax
import jax.numpy as jnp
from jax import lax
from jax.experimental import pallas as pl
from jax.experimental.pallas import tpu as pltpu
from jax.sharding import PartitionSpec as P

KERNEL_VMEM = 1 << 20


def prepare_kernel(
    kept_hbm,
    mask_hbm,
    owner_hbm,
    amp_hbm,
    integrals_hbm,
    residual_hbm,
    pair_hbm,
    virt_hbm,
    rows_ref,
    own_ref,
    residual_ref,
    under_ref,
    kept_ref,
    mask_ref,
    owner_ref,
    amp_ref,
    rest_ref,
    pair_ref,
    virt_ref,
    kept_rows_ref,
    sems,
):
    moves = [
        pltpu.make_async_copy(source, target, sems.at[n])
        for n, (source, target) in enumerate(
            (
                (kept_hbm, kept_ref),
                (mask_hbm, mask_ref),
                (owner_hbm, owner_ref),
                (amp_hbm, amp_ref),
                (integrals_hbm, own_ref.at[0]),
                (residual_hbm, rest_ref),
                (pair_hbm, pair_ref),
                (virt_hbm, virt_ref),
            )
        )
    ]
    for move in moves:
        move.start()
    blocks, keep, pair_rows, width = amp_ref.shape
    tiles = mask_ref.shape[1]
    tasks = blocks * keep
    own_rows = rows_ref.shape[1]
    count = rows_ref.shape[2] // width
    me = lax.axis_index("pair")
    lane_tile = lax.broadcasted_iota(jnp.int32, (pair_rows, width), 1) // (width // tiles)
    row = lax.broadcasted_iota(jnp.int32, (count * own_rows, tasks * pair_rows), 0)
    column = lax.broadcasted_iota(jnp.int32, (count * own_rows, tasks * pair_rows), 1)
    wanted = jnp.full(row.shape, -1, jnp.int32)
    for move in moves:
        move.wait()
    for b in range(blocks):
        for k in range(keep):
            task = b * keep + k
            first = ((owner_ref[kept_ref[b, k]] ^ me) * blocks + b) * pair_rows
            wanted = jnp.where(column // pair_rows == task, first + column % pair_rows, wanted)
            scale = jnp.zeros((pair_rows, width), jnp.float32)
            for s in range(tiles):
                scale = jnp.where(lane_tile == s, mask_ref[b, s, k].astype(jnp.float32), scale)
            kept_rows_ref[pl.ds(task * pair_rows, pair_rows), :] = amp_ref[b, k].astype(jnp.float32) * scale
    pick = (row == wanted).astype(jnp.bfloat16)
    spread = jnp.dot(pick, kept_rows_ref[...].astype(jnp.bfloat16), preferred_element_type=jnp.float32)
    for t in range(count):
        rows_ref[0, :, t * width : (t + 1) * width] = spread[t * own_rows : (t + 1) * own_rows].astype(rows_ref.dtype)
    residual_ref[...] = rest_ref[...].astype(jnp.float32)
    count = under_ref.shape[0]
    here = lax.broadcasted_iota(jnp.int32, (count, count), 0)
    there = lax.broadcasted_iota(jnp.int32, (count, count), 1)
    pair_column = jnp.sum(jnp.where(here == there, pair_ref[...], 0.0), axis=1, keepdims=True)
    under_ref[...] = pair_column - virt_ref[...]


def prepare(amplitudes, kept_groups, tile_mask, owner_table, integrals, residual_in, pair_energy, virt_energy):
    blocks, keep, pair_rows, width = amplitudes.shape
    rows_shape = (1, blocks * pair_rows, owner_table.shape[0] * width)
    operands = (
        kept_groups,
        jnp.swapaxes(tile_mask, 1, 2),
        owner_table,
        amplitudes,
        integrals,
        residual_in,
        pair_energy[None, :],
        virt_energy[None, :],
    )
    operands = [pltpu.with_memory_space_constraint(x, pltpu.HBM) for x in operands]
    scratch = [pltpu.SMEM(x.shape, x.dtype) for x in operands[:3]]
    scratch += [pltpu.VMEM(x.shape, x.dtype) for x in (operands[3], *operands[5:])]
    return pl.pallas_call(
        prepare_kernel,
        out_shape=[
            jax.ShapeDtypeStruct(rows_shape, amplitudes.dtype),
            jax.ShapeDtypeStruct((1, *integrals.shape), integrals.dtype),
            jax.ShapeDtypeStruct(residual_in.shape, jnp.float32),
            jax.ShapeDtypeStruct(residual_in.shape, jnp.float32),
        ],
        in_specs=[pl.BlockSpec(memory_space=pl.ANY)] * len(operands),
        out_specs=[pl.BlockSpec(memory_space=pltpu.VMEM)] * 4,
        scratch_shapes=scratch
        + [pltpu.VMEM((blocks * keep * pair_rows, width), jnp.float32), pltpu.SemaphoreType.DMA((len(operands),))],
        compiler_params=pltpu.CompilerParams(vmem_limit_bytes=KERNEL_VMEM),
        name="prepare",
    )(*operands)


def update_kernel(
    blocks, pair_rows, order, places, first_ref, more_ref, residual_ref, under_ref, *refs
):
    *integral_refs, out_ref, sorted_ref, rows_ref = refs
    width = integral_refs[0].shape[1]
    full_rows = len(order) * pair_rows
    me = lax.axis_index("virt")
    pieces = [first_ref[n] for n in range(first_ref.shape[0])]
    pieces += [more_ref[n] for n in range(more_ref.shape[0])]
    for mask, piece in zip(order, pieces):
        sorted_ref[me ^ mask] = piece.astype(jnp.float32)
    for v in range(len(order)):
        for b in range(blocks):
            rows_ref[pl.ds(b * full_rows + v * pair_rows, pair_rows), :] = sorted_ref[
                v, pl.ds(b * pair_rows, pair_rows), :
            ]
    rows = rows_ref[...].astype(jnp.bfloat16)
    total = residual_ref[...]
    for ref, at in zip(integral_refs, places):
        for n, place in enumerate(at):
            total += jnp.dot(
                rows[:, place * width : (place + 1) * width], ref[n], preferred_element_type=jnp.float32
            )
    out_ref[...] = total / under_ref[...]


def swap(x, pair_mask, virt_mask):
    pair_size, virt_size = lax.axis_size("pair"), lax.axis_size("virt")
    moves = [
        (p * virt_size + v, (p ^ pair_mask) * virt_size + (v ^ virt_mask))
        for p in range(pair_size)
        for v in range(virt_size)
    ]
    return lax.ppermute(x, ("pair", "virt"), moves)


def local(
    amplitudes,
    kept_groups,
    tile_mask,
    owner_table,
    integrals,
    residual_in,
    pair_energy,
    virt_energy,
):
    blocks, _, pair_rows, _ = amplitudes.shape
    vmem = pl.BlockSpec(memory_space=pltpu.VMEM)
    virt_size = lax.axis_size("virt")

    diagonal = swap(integrals[None], 3, 0)
    far = swap(integrals[None], 4, 0)

    rows, own, residual, under = prepare(
        amplitudes, kept_groups, tile_mask, owner_table, integrals, residual_in, pair_energy, virt_energy
    )
    pieces, order, more = rows, [0], None
    for bit in range((virt_size - 1).bit_length()):
        if more is not None:
            pieces = jnp.concatenate([pieces, more], axis=0)
        more = swap(pieces, 0, 1 << bit)
        order = order + [at ^ (1 << bit) for at in order]

    both = jnp.concatenate([own, far], axis=0)
    arrays = [(own, (0,)), (diagonal, (3,)), (far, (4,)), (swap(far, 3, 0), (7,))]
    arrays += [(swap(both, mask, 0), (mask, mask ^ 4)) for mask in (2, 1)]
    return pl.pallas_call(
        functools.partial(update_kernel, blocks, pair_rows, order, [at for _, at in arrays]),
        out_shape=jax.ShapeDtypeStruct(residual_in.shape, jnp.float32),
        in_specs=[vmem] * (4 + len(arrays)),
        out_specs=vmem,
        scratch_shapes=[
            pltpu.VMEM((virt_size, *pieces.shape[1:]), jnp.float32),
            pltpu.VMEM((residual_in.shape[0], pieces.shape[2]), jnp.float32),
        ],
        compiler_params=pltpu.CompilerParams(vmem_limit_bytes=KERNEL_VMEM),
        name="update",
    )(pieces, more, residual, under, *[x for x, _ in arrays])


def general(
    amplitudes,
    kept_groups,
    tile_mask,
    owner_table,
    integrals,
    residual_in,
    pair_energy,
    virt_energy,
):
    block_count = amplitudes.shape[0]
    keep_count = amplitudes.shape[1]
    pair_rows = amplitudes.shape[2]
    group_width = amplitudes.shape[3]
    column_count = integrals.shape[1]
    tile_width = group_width // tile_mask.shape[2]
    group_total = owner_table.shape[0]
    tile_keep = jnp.repeat(tile_mask.astype(amplitudes.dtype), tile_width, axis=2)
    kept_amplitudes = amplitudes * tile_keep[:, :, None, :]
    group_match = kept_groups[:, :, None] == jnp.arange(group_total, dtype=jnp.int32)[None, None, :]
    owner_slots = jnp.sum(jnp.where(group_match, owner_table[None, None, :], 0), axis=2)
    placing = owner_slots[:, None, :] == jnp.arange(group_total, dtype=jnp.int32)[None, :, None]
    outgoing = jnp.einsum(
        "bqk,bkrw->qbrw", placing.astype(jnp.bfloat16), kept_amplitudes, preferred_element_type=jnp.float32
    ).astype(jnp.bfloat16)
    full_pairs = pair_rows * lax.axis_size("virt")
    arrived = lax.all_to_all(outgoing, "pair", split_axis=0, concat_axis=0, tiled=True)
    assembled = lax.all_gather(arrived, "virt", axis=2, tiled=True)
    partial_value = jnp.dot(
        assembled.reshape(-1, group_width), integrals, preferred_element_type=jnp.float32
    )
    ladder = lax.psum_scatter(partial_value, "pair", scatter_dimension=0, tiled=True)
    denominator = pair_energy[:, None] - virt_energy[None, :]
    return (residual_in.astype(jnp.float32) + ladder) / denominator


def solution(mesh):
    pair_size, virt_size = mesh.shape["pair"], mesh.shape["virt"]
    regular = pair_size == 8 and virt_size in (2, 4, 8)
    return jax.shard_map(
        local if regular else general,
        mesh=mesh,
        in_specs=(
            P("pair", None, "virt", None),
            P("pair", None),
            P("pair", None, None),
            P(),
            P("pair", "virt"),
            P("pair", "virt"),
            P("pair"),
            P("virt"),
        ),
        out_specs=P("pair", "virt"),
        check_vma=False,
    )
```

```python
import functools

import jax
import jax.numpy as jnp
from jax import lax
from jax.experimental import pallas as pl
from jax.experimental.pallas import tpu as pltpu
from jax.sharding import PartitionSpec as P

KERNEL_VMEM = 1 << 20


def prepare_kernel(
    kept_hbm,
    mask_hbm,
    owner_hbm,
    amp_hbm,
    integrals_hbm,
    residual_hbm,
    pair_hbm,
    virt_hbm,
    rows_ref,
    own_ref,
    residual_ref,
    under_ref,
    kept_ref,
    mask_ref,
    owner_ref,
    amp_ref,
    rest_ref,
    pair_ref,
    virt_ref,
    kept_rows_ref,
    sems,
):
    moves = [
        pltpu.make_async_copy(source, target, sems.at[n])
        for n, (source, target) in enumerate(
            (
                (kept_hbm, kept_ref),
                (mask_hbm, mask_ref),
                (owner_hbm, owner_ref),
                (amp_hbm, amp_ref),
                (integrals_hbm, own_ref.at[0]),
                (residual_hbm, rest_ref),
                (pair_hbm, pair_ref),
                (virt_hbm, virt_ref),
            )
        )
    ]
    for move in moves:
        move.start()
    blocks, keep, pair_rows, width = amp_ref.shape
    tiles = mask_ref.shape[1]
    tasks = blocks * keep
    own_rows = rows_ref.shape[1]
    count = rows_ref.shape[2] // width
    me = lax.axis_index("pair")
    lane_tile = lax.broadcasted_iota(jnp.int32, (pair_rows, width), 1) // (width // tiles)
    row = lax.broadcasted_iota(jnp.int32, (count * own_rows, tasks * pair_rows), 0)
    column = lax.broadcasted_iota(jnp.int32, (count * own_rows, tasks * pair_rows), 1)
    wanted = jnp.full(row.shape, -1, jnp.int32)
    for move in moves:
        move.wait()
    for b in range(blocks):
        for k in range(keep):
            task = b * keep + k
            first = ((owner_ref[kept_ref[b, k]] ^ me) * blocks + b) * pair_rows
            wanted = jnp.where(column // pair_rows == task, first + column % pair_rows, wanted)
            scale = jnp.zeros((pair_rows, width), jnp.float32)
            for s in range(tiles):
                scale = jnp.where(lane_tile == s, mask_ref[b, s, k].astype(jnp.float32), scale)
            kept_rows_ref[pl.ds(task * pair_rows, pair_rows), :] = amp_ref[b, k].astype(jnp.float32) * scale
    pick = (row == wanted).astype(jnp.bfloat16)
    spread = jnp.dot(pick, kept_rows_ref[...].astype(jnp.bfloat16), preferred_element_type=jnp.float32)
    for t in range(count):
        rows_ref[0, :, t * width : (t + 1) * width] = spread[t * own_rows : (t + 1) * own_rows].astype(rows_ref.dtype)
    residual_ref[...] = rest_ref[...].astype(jnp.float32)
    count = under_ref.shape[0]
    here = lax.broadcasted_iota(jnp.int32, (count, count), 0)
    there = lax.broadcasted_iota(jnp.int32, (count, count), 1)
    pair_column = jnp.sum(jnp.where(here == there, pair_ref[...], 0.0), axis=1, keepdims=True)
    under_ref[...] = pair_column - virt_ref[...]


def prepare(amplitudes, kept_groups, tile_mask, owner_table, integrals, residual_in, pair_energy, virt_energy):
    blocks, keep, pair_rows, width = amplitudes.shape
    rows_shape = (1, blocks * pair_rows, owner_table.shape[0] * width)
    operands = (
        kept_groups,
        jnp.swapaxes(tile_mask, 1, 2),
        owner_table,
        amplitudes,
        integrals,
        residual_in,
        pair_energy[None, :],
        virt_energy[None, :],
    )
    operands = [pltpu.with_memory_space_constraint(x, pltpu.HBM) for x in operands]
    scratch = [pltpu.SMEM(x.shape, x.dtype) for x in operands[:3]]
    scratch += [pltpu.VMEM(x.shape, x.dtype) for x in (operands[3], *operands[5:])]
    return pl.pallas_call(
        prepare_kernel,
        out_shape=[
            jax.ShapeDtypeStruct(rows_shape, amplitudes.dtype),
            jax.ShapeDtypeStruct((1, *integrals.shape), integrals.dtype),
            jax.ShapeDtypeStruct(residual_in.shape, jnp.float32),
            jax.ShapeDtypeStruct(residual_in.shape, jnp.float32),
        ],
        in_specs=[pl.BlockSpec(memory_space=pl.ANY)] * len(operands),
        out_specs=[pl.BlockSpec(memory_space=pltpu.VMEM)] * 4,
        scratch_shapes=scratch
        + [pltpu.VMEM((blocks * keep * pair_rows, width), jnp.float32), pltpu.SemaphoreType.DMA((len(operands),))],
        compiler_params=pltpu.CompilerParams(vmem_limit_bytes=KERNEL_VMEM),
        name="prepare",
    )(*operands)


def update_kernel(
    blocks, pair_rows, order, places, *refs
):
    *integral_refs, first_ref, more_ref, residual_ref, under_ref, out_ref, sorted_ref, rows_ref = refs
    width = integral_refs[0].shape[1]
    full_rows = len(order) * pair_rows
    me = lax.axis_index("virt")
    pieces = [first_ref[n] for n in range(first_ref.shape[0])]
    pieces += [more_ref[n] for n in range(more_ref.shape[0])]
    for mask, piece in zip(order, pieces):
        sorted_ref[me ^ mask] = piece.astype(jnp.float32)
    for v in range(len(order)):
        for b in range(blocks):
            rows_ref[pl.ds(b * full_rows + v * pair_rows, pair_rows), :] = sorted_ref[
                v, pl.ds(b * pair_rows, pair_rows), :
            ]
    rows = rows_ref[...].astype(jnp.bfloat16)
    total = residual_ref[...]
    for ref, at in zip(integral_refs, places):
        for n, place in enumerate(at):
            total += jnp.dot(
                rows[:, place * width : (place + 1) * width], ref[n], preferred_element_type=jnp.float32
            )
    out_ref[...] = total / under_ref[...]


def swap(x, pair_mask, virt_mask):
    pair_size, virt_size = lax.axis_size("pair"), lax.axis_size("virt")
    moves = [
        (p * virt_size + v, (p ^ pair_mask) * virt_size + (v ^ virt_mask))
        for p in range(pair_size)
        for v in range(virt_size)
    ]
    return lax.ppermute(x, ("pair", "virt"), moves)


def local(
    amplitudes,
    kept_groups,
    tile_mask,
    owner_table,
    integrals,
    residual_in,
    pair_energy,
    virt_energy,
):
    blocks, _, pair_rows, _ = amplitudes.shape
    vmem = pl.BlockSpec(memory_space=pltpu.VMEM)
    virt_size = lax.axis_size("virt")

    diagonal = swap(integrals[None], 3, 0)
    far = swap(integrals[None], 4, 0)

    rows, own, residual, under = prepare(
        amplitudes, kept_groups, tile_mask, owner_table, integrals, residual_in, pair_energy, virt_energy
    )
    pieces, order, more = rows, [0], None
    for bit in range((virt_size - 1).bit_length()):
        if more is not None:
            pieces = jnp.concatenate([pieces, more], axis=0)
        mask = (1 << bit) | 1
        more = swap(pieces, 0, mask)
        order = order + [at ^ mask for at in order]

    both = jnp.concatenate([own, far], axis=0)
    along_x = swap(both, 1, 0)
    beyond = swap(far, 3, 0)
    along_z = swap(both, 2, 0)
    arrays = [(along_z, (2, 6)), (own, (0,)), (diagonal, (3,)), (far, (4,)), (beyond, (7,)), (along_x, (1, 5))]
    return pl.pallas_call(
        functools.partial(update_kernel, blocks, pair_rows, order, [at for _, at in arrays]),
        out_shape=jax.ShapeDtypeStruct(residual_in.shape, jnp.float32),
        in_specs=[vmem] * (4 + len(arrays)),
        out_specs=vmem,
        scratch_shapes=[
            pltpu.VMEM((virt_size, *pieces.shape[1:]), jnp.float32),
            pltpu.VMEM((residual_in.shape[0], pieces.shape[2]), jnp.float32),
        ],
        compiler_params=pltpu.CompilerParams(vmem_limit_bytes=KERNEL_VMEM),
        name="update",
    )(*[x for x, _ in arrays], pieces, more, residual, under)


def general(
    amplitudes,
    kept_groups,
    tile_mask,
    owner_table,
    integrals,
    residual_in,
    pair_energy,
    virt_energy,
):
    block_count = amplitudes.shape[0]
    keep_count = amplitudes.shape[1]
    pair_rows = amplitudes.shape[2]
    group_width = amplitudes.shape[3]
    column_count = integrals.shape[1]
    tile_width = group_width // tile_mask.shape[2]
    group_total = owner_table.shape[0]
    tile_keep = jnp.repeat(tile_mask.astype(amplitudes.dtype), tile_width, axis=2)
    kept_amplitudes = amplitudes * tile_keep[:, :, None, :]
    group_match = kept_groups[:, :, None] == jnp.arange(group_total, dtype=jnp.int32)[None, None, :]
    owner_slots = jnp.sum(jnp.where(group_match, owner_table[None, None, :], 0), axis=2)
    placing = owner_slots[:, None, :] == jnp.arange(group_total, dtype=jnp.int32)[None, :, None]
    outgoing = jnp.einsum(
        "bqk,bkrw->qbrw", placing.astype(jnp.bfloat16), kept_amplitudes, preferred_element_type=jnp.float32
    ).astype(jnp.bfloat16)
    full_pairs = pair_rows * lax.axis_size("virt")
    arrived = lax.all_to_all(outgoing, "pair", split_axis=0, concat_axis=0, tiled=True)
    assembled = lax.all_gather(arrived, "virt", axis=2, tiled=True)
    partial_value = jnp.dot(
        assembled.reshape(-1, group_width), integrals, preferred_element_type=jnp.float32
    )
    ladder = lax.psum_scatter(partial_value, "pair", scatter_dimension=0, tiled=True)
    denominator = pair_energy[:, None] - virt_energy[None, :]
    return (residual_in.astype(jnp.float32) + ladder) / denominator


def solution(mesh):
    pair_size, virt_size = mesh.shape["pair"], mesh.shape["virt"]
    regular = pair_size == 8 and virt_size in (2, 4, 8)
    return jax.shard_map(
        local if regular else general,
        mesh=mesh,
        in_specs=(
            P("pair", None, "virt", None),
            P("pair", None),
            P("pair", None, None),
            P(),
            P("pair", "virt"),
            P("pair", "virt"),
            P("pair"),
            P("virt"),
        ),
        out_specs=P("pair", "virt"),
        check_vma=False,
    )
```

```python
import functools

import jax
import jax.numpy as jnp
from jax import lax
from jax.experimental import pallas as pl
from jax.experimental.pallas import tpu as pltpu
from jax.sharding import PartitionSpec as P

KERNEL_VMEM = 1 << 20


def prepare_kernel(
    kept_hbm,
    mask_hbm,
    owner_hbm,
    amp_hbm,
    integrals_hbm,
    residual_hbm,
    pair_hbm,
    virt_hbm,
    rows_ref,
    own_ref,
    residual_ref,
    under_ref,
    kept_ref,
    mask_ref,
    owner_ref,
    amp_ref,
    rest_ref,
    pair_ref,
    virt_ref,
    kept_rows_ref,
    sems,
):
    moves = [
        pltpu.make_async_copy(source, target, sems.at[n])
        for n, (source, target) in enumerate(
            (
                (kept_hbm, kept_ref),
                (mask_hbm, mask_ref),
                (owner_hbm, owner_ref),
                (amp_hbm, amp_ref),
                (integrals_hbm, own_ref.at[0]),
                (residual_hbm, rest_ref),
                (pair_hbm, pair_ref),
                (virt_hbm, virt_ref),
            )
        )
    ]
    for move in moves:
        move.start()
    blocks, keep, pair_rows, width = amp_ref.shape
    tiles = mask_ref.shape[1]
    tasks = blocks * keep
    own_rows = rows_ref.shape[1]
    count = rows_ref.shape[2] // width
    me = lax.axis_index("pair")
    lane_tile = lax.broadcasted_iota(jnp.int32, (pair_rows, width), 1) // (width // tiles)
    row = lax.broadcasted_iota(jnp.int32, (count * own_rows, tasks * pair_rows), 0)
    column = lax.broadcasted_iota(jnp.int32, (count * own_rows, tasks * pair_rows), 1)
    wanted = jnp.full(row.shape, -1, jnp.int32)
    for move in moves:
        move.wait()
    for b in range(blocks):
        for k in range(keep):
            task = b * keep + k
            first = ((owner_ref[kept_ref[b, k]] ^ me) * blocks + b) * pair_rows
            wanted = jnp.where(column // pair_rows == task, first + column % pair_rows, wanted)
            scale = jnp.zeros((pair_rows, width), jnp.float32)
            for s in range(tiles):
                scale = jnp.where(lane_tile == s, mask_ref[b, s, k].astype(jnp.float32), scale)
            kept_rows_ref[pl.ds(task * pair_rows, pair_rows), :] = amp_ref[b, k].astype(jnp.float32) * scale
    pick = (row == wanted).astype(jnp.bfloat16)
    spread = jnp.dot(pick, kept_rows_ref[...].astype(jnp.bfloat16), preferred_element_type=jnp.float32)
    for t in range(count):
        rows_ref[0, :, t * width : (t + 1) * width] = spread[t * own_rows : (t + 1) * own_rows].astype(rows_ref.dtype)
    residual_ref[...] = rest_ref[...].astype(jnp.float32)
    count = under_ref.shape[0]
    here = lax.broadcasted_iota(jnp.int32, (count, count), 0)
    there = lax.broadcasted_iota(jnp.int32, (count, count), 1)
    pair_column = jnp.sum(jnp.where(here == there, pair_ref[...], 0.0), axis=1, keepdims=True)
    under_ref[...] = pair_column - virt_ref[...]


def prepare(amplitudes, kept_groups, tile_mask, owner_table, integrals, residual_in, pair_energy, virt_energy):
    blocks, keep, pair_rows, width = amplitudes.shape
    rows_shape = (1, blocks * pair_rows, owner_table.shape[0] * width)
    operands = (
        kept_groups,
        jnp.swapaxes(tile_mask, 1, 2),
        owner_table,
        amplitudes,
        integrals,
        residual_in,
        pair_energy[None, :],
        virt_energy[None, :],
    )
    operands = [pltpu.with_memory_space_constraint(x, pltpu.HBM) for x in operands]
    scratch = [pltpu.SMEM(x.shape, x.dtype) for x in operands[:3]]
    scratch += [pltpu.VMEM(x.shape, x.dtype) for x in (operands[3], *operands[5:])]
    return pl.pallas_call(
        prepare_kernel,
        out_shape=[
            jax.ShapeDtypeStruct(rows_shape, amplitudes.dtype),
            jax.ShapeDtypeStruct((1, *integrals.shape), integrals.dtype),
            jax.ShapeDtypeStruct(residual_in.shape, jnp.float32),
            jax.ShapeDtypeStruct(residual_in.shape, jnp.float32),
        ],
        in_specs=[pl.BlockSpec(memory_space=pl.ANY)] * len(operands),
        out_specs=[pl.BlockSpec(memory_space=pltpu.VMEM)] * 4,
        scratch_shapes=scratch
        + [pltpu.VMEM((blocks * keep * pair_rows, width), jnp.float32), pltpu.SemaphoreType.DMA((len(operands),))],
        compiler_params=pltpu.CompilerParams(vmem_limit_bytes=KERNEL_VMEM),
        name="prepare",
    )(*operands)


def update_kernel(
    blocks, pair_rows, order, places, *refs
):
    *integral_refs, first_ref, more_ref, residual_ref, under_ref, out_ref, sorted_ref, rows_ref = refs
    width = integral_refs[0].shape[1]
    full_rows = len(order) * pair_rows
    me = lax.axis_index("virt")
    pieces = [first_ref[n] for n in range(first_ref.shape[0])]
    pieces += [more_ref[n] for n in range(more_ref.shape[0])]
    for mask, piece in zip(order, pieces):
        sorted_ref[me ^ mask] = piece.astype(jnp.float32)
    for v in range(len(order)):
        for b in range(blocks):
            rows_ref[pl.ds(b * full_rows + v * pair_rows, pair_rows), :] = sorted_ref[
                v, pl.ds(b * pair_rows, pair_rows), :
            ]
    rows = rows_ref[...].astype(jnp.bfloat16)
    total = residual_ref[...]
    for ref, at in zip(integral_refs, places):
        for n, place in enumerate(at):
            total += jnp.dot(
                rows[:, place * width : (place + 1) * width], ref[n], preferred_element_type=jnp.float32
            )
    out_ref[...] = total / under_ref[...]


def swap(x, pair_mask, virt_mask):
    pair_size, virt_size = lax.axis_size("pair"), lax.axis_size("virt")
    moves = [
        (p * virt_size + v, (p ^ pair_mask) * virt_size + (v ^ virt_mask))
        for p in range(pair_size)
        for v in range(virt_size)
    ]
    return lax.ppermute(x, ("pair", "virt"), moves)


def local(
    amplitudes,
    kept_groups,
    tile_mask,
    owner_table,
    integrals,
    residual_in,
    pair_energy,
    virt_energy,
):
    blocks, _, pair_rows, _ = amplitudes.shape
    vmem = pl.BlockSpec(memory_space=pltpu.VMEM)
    virt_size = lax.axis_size("virt")

    diagonal = swap(integrals[None], 3, 0)
    far = swap(integrals[None], 4, 0)

    rows, own, residual, under = prepare(
        amplitudes, kept_groups, tile_mask, owner_table, integrals, residual_in, pair_energy, virt_energy
    )
    pieces, order, more = rows, [0], None
    for bit in range((virt_size - 1).bit_length()):
        if more is not None:
            pieces = jnp.concatenate([pieces, more], axis=0)
        mask = (1 << bit) | 1
        more = swap(pieces, 0, mask)
        order = order + [at ^ mask for at in order]

    both = jnp.concatenate([own, far], axis=0)
    beyond = swap(far, 3, 0)
    along_z = swap(both, 2, 0)
    along_x = swap(both, 1, 0)
    arrays = [(far, (4,)), (beyond, (7,)), (along_z, (2, 6)), (own, (0,)), (along_x, (1, 5)), (diagonal, (3,))]
    return pl.pallas_call(
        functools.partial(update_kernel, blocks, pair_rows, order, [at for _, at in arrays]),
        out_shape=jax.ShapeDtypeStruct(residual_in.shape, jnp.float32),
        in_specs=[vmem] * (4 + len(arrays)),
        out_specs=vmem,
        scratch_shapes=[
            pltpu.VMEM((virt_size, *pieces.shape[1:]), jnp.float32),
            pltpu.VMEM((residual_in.shape[0], pieces.shape[2]), jnp.float32),
        ],
        compiler_params=pltpu.CompilerParams(vmem_limit_bytes=KERNEL_VMEM),
        name="update",
    )(*[x for x, _ in arrays], pieces, more, residual, under)


def general(
    amplitudes,
    kept_groups,
    tile_mask,
    owner_table,
    integrals,
    residual_in,
    pair_energy,
    virt_energy,
):
    block_count = amplitudes.shape[0]
    keep_count = amplitudes.shape[1]
    pair_rows = amplitudes.shape[2]
    group_width = amplitudes.shape[3]
    column_count = integrals.shape[1]
    tile_width = group_width // tile_mask.shape[2]
    group_total = owner_table.shape[0]
    tile_keep = jnp.repeat(tile_mask.astype(amplitudes.dtype), tile_width, axis=2)
    kept_amplitudes = amplitudes * tile_keep[:, :, None, :]
    group_match = kept_groups[:, :, None] == jnp.arange(group_total, dtype=jnp.int32)[None, None, :]
    owner_slots = jnp.sum(jnp.where(group_match, owner_table[None, None, :], 0), axis=2)
    placing = owner_slots[:, None, :] == jnp.arange(group_total, dtype=jnp.int32)[None, :, None]
    outgoing = jnp.einsum(
        "bqk,bkrw->qbrw", placing.astype(jnp.bfloat16), kept_amplitudes, preferred_element_type=jnp.float32
    ).astype(jnp.bfloat16)
    full_pairs = pair_rows * lax.axis_size("virt")
    arrived = lax.all_to_all(outgoing, "pair", split_axis=0, concat_axis=0, tiled=True)
    assembled = lax.all_gather(arrived, "virt", axis=2, tiled=True)
    partial_value = jnp.dot(
        assembled.reshape(-1, group_width), integrals, preferred_element_type=jnp.float32
    )
    ladder = lax.psum_scatter(partial_value, "pair", scatter_dimension=0, tiled=True)
    denominator = pair_energy[:, None] - virt_energy[None, :]
    return (residual_in.astype(jnp.float32) + ladder) / denominator


def solution(mesh):
    pair_size, virt_size = mesh.shape["pair"], mesh.shape["virt"]
    regular = pair_size == 8 and virt_size in (2, 4, 8)
    return jax.shard_map(
        local if regular else general,
        mesh=mesh,
        in_specs=(
            P("pair", None, "virt", None),
            P("pair", None),
            P("pair", None, None),
            P(),
            P("pair", "virt"),
            P("pair", "virt"),
            P("pair"),
            P("virt"),
        ),
        out_specs=P("pair", "virt"),
        check_vma=False,
    )
```
